128 devices in a mesh: ctx: 32 (over z, y_hi, x), wa: 4 (over y_lo, core).
Axes of the slice: x: 4, y: 4 (y_hi: 2, y_lo: 2; y = y_hi * 2 + y_lo), z: 4, core: 2. Of those that a mesh axis runs over, the one named last changes fastest.
Arguments:
- tokens: bfloat16 [4096, 8192], P('ctx', 'wa')
- norm_gain: bfloat16 [8192], P('wa'), may hold values from 0.5 to 1.5
- w_query: bfloat16 [8192, 4096], P('wa'), may hold values from -0.0625 to 0.0625
- keyvalue_weight: bfloat16 [8192, 1024], P('wa'), may hold values from -0.0625 to 0.0625
- cache_keyval: bfloat16 [65536, 1024], P('ctx', 'wa')
- kept_blocks: int32 [32, 3], P('ctx'), may hold values from 0 to 15, as said below
- kept_counts: int32 [32], P('ctx'), may hold values from 1 to 3, as said below
Outputs:
- attended: bfloat16 [4096, 4096], P('ctx', 'wa')
The draws below stay inside these ranges and needn't reach their ends.
Inputs may be any that keep to these rules, and one draw needn't show every extreme that they name: `kept_blocks`: within one row the indices are distinct. `kept_counts`: some shard uses exactly 3 slots.
All inputs are finite; a program needn't handle non-finite values.
Results may differ from the reference program's by a relative error of at most 0.0095.
The reference program's roundings to bfloat16 on the way (of `normed`, `queries`, `new_keyval` and `weights`) count: a program that leaves them out, or rounds other values in their place, can miss the bound.
Values may be sent and summed in bfloat16 or wider, within the bound.
No kernel may reach another device: no remote copies, remote signals or barrier semaphores. Data moves between devices by JAX's collectives and lax.ppermute only.
A program may use at most 192 MiB of HBM per device.

```python
import jax
import jax.numpy as jnp
from jax import lax

MODEL_WIDTH = 8192
QUERY_HEADS = 32
KEYVALUE_HEADS = 4
HEAD_WIDTH = 128
BLOCK = 128
MAXB = 3
TOK_DEV = 128
SHARDS = 32
TOKENS = 4096
CONTEXT_LENGTH = 65536
NB = 16


def draw_tokens(key, part):
    key = jax.random.fold_in(key, 3)
    leading_key, following_key = jax.random.split(key, 2)
    sample_draws = jax.random.normal(leading_key, (TOKENS, MODEL_WIDTH), jnp.float32)
    row_scale = 10.0 ** jax.random.uniform(following_key, (TOKENS, 1), jnp.float32, -0.5, 0.5)
    col_scale = 10.0 ** (jnp.arange(MODEL_WIDTH).astype(jnp.float32) / MODEL_WIDTH - 0.5)
    return (sample_draws * row_scale * col_scale[None, :]).astype(jnp.bfloat16)


def draw_cache_keyval(key, part):
    key = jax.random.fold_in(key, 5)
    leading_key = jax.random.fold_in(key, 0)
    sample_draws = jax.random.normal(leading_key, (CONTEXT_LENGTH, KEYVALUE_HEADS, 2, HEAD_WIDTH), jnp.float32)
    return sample_draws.reshape(CONTEXT_LENGTH, KEYVALUE_HEADS * 2 * HEAD_WIDTH).astype(jnp.bfloat16)


def kept_common(key):
    own_key = jax.random.fold_in(key, 7)
    count_key, top_key, order_key = jax.random.split(own_key, 3)
    counts = jax.random.randint(count_key, (SHARDS,), 1, MAXB + 1)
    busiest = jax.random.randint(top_key, (), 0, SHARDS)
    counts = jnp.where(jnp.arange(SHARDS) == busiest, MAXB, counts)
    ranking = jax.random.randint(order_key, (SHARDS, NB), 0, 1 << 20) * NB + jnp.arange(NB)[None, :]
    orders = jnp.argsort(ranking, axis=1)[:, :MAXB]
    return (orders.astype(jnp.int32), counts.astype(jnp.int32))


def draw_kept_blocks(key, part):
    return kept_common(key)[0]


def draw_kept_counts(key, part):
    return kept_common(key)[1]


def levels(rng, dims, shards, smallest, high):
    loudness = 1.0
    for dim, parts in shards:
        heights = jax.random.uniform(jax.random.fold_in(jax.random.fold_in(rng, 6), dim), (parts,), jnp.float32, smallest / len(shards), high / len(shards))
        loudness = loudness * jnp.repeat(jnp.exp(heights), dims[dim] // parts).reshape((-1,) + (1,) * (len(dims) - 1 - dim))
    return loudness


def noise(stream_key, shape, spread, limit, shards=(), dtype=jnp.bfloat16):
    factor_of = levels(stream_key, shape, shards, -0.22, 0.18) if shards else 1.0
    entries = jax.random.normal(stream_key, shape, jnp.float32) * spread * factor_of
    return jnp.minimum(jnp.maximum(entries, -limit), limit).astype(dtype)


def setup_inputs(seed: int = 0) -> dict:
    key_list = jax.random.split(jax.random.key(seed), 8)
    tokens = draw_tokens(jax.random.fold_in(key_list[7], 71), 0)
    norm_gain = jnp.clip(1.0 + 0.1 * jax.random.normal(key_list[1], (MODEL_WIDTH,), jnp.float32), 0.5, 1.5).astype(jnp.bfloat16)
    w_query = noise(key_list[2], (MODEL_WIDTH, QUERY_HEADS * HEAD_WIDTH), MODEL_WIDTH ** -0.5, 0.0625, ((0, 4),))
    keyvalue_weight = noise(key_list[3], (MODEL_WIDTH, KEYVALUE_HEADS * 2 * HEAD_WIDTH), MODEL_WIDTH ** -0.5, 0.0625, ((0, 4),))
    cache_keyval = draw_cache_keyval(jax.random.fold_in(key_list[7], 71), 0)
    kept_blocks = draw_kept_blocks(jax.random.fold_in(key_list[7], 71), 0)
    kept_counts = draw_kept_counts(jax.random.fold_in(key_list[7], 71), 0)
    return {"tokens": tokens, "norm_gain": norm_gain, "w_query": w_query, "keyvalue_weight": keyvalue_weight, "cache_keyval": cache_keyval, "kept_blocks": kept_blocks, "kept_counts": kept_counts}


def rms_normed(tokens, norm_gain):
    values = tokens.astype(jnp.float32)
    meansq = lax.optimization_barrier(jnp.mean(values * values, axis=1, keepdims=True))
    return (values * lax.rsqrt(meansq + 1e-05) * norm_gain.astype(jnp.float32)[None, :]).astype(jnp.bfloat16)

def reference(tokens, norm_gain, w_query, keyvalue_weight, cache_keyval, kept_blocks, kept_counts):
    normed = rms_normed(tokens, norm_gain)
    queries = (jnp.dot(normed, w_query, preferred_element_type=jnp.float32) * HEAD_WIDTH ** (-0.5)).astype(jnp.bfloat16)
    new_keyval = jnp.dot(normed, keyvalue_weight, preferred_element_type=jnp.float32).astype(jnp.bfloat16)
    width_value = KEYVALUE_HEADS * 2 * HEAD_WIDTH
    cache_four = cache_keyval.reshape(SHARDS, NB, BLOCK, width_value)
    picked = cache_four[jnp.arange(SHARDS).astype(jnp.int32)[:, None], kept_blocks]
    kept_rows = picked.reshape(SHARDS * MAXB * BLOCK, width_value)
    slot_live = jnp.arange(MAXB).astype(jnp.int32)[None, :] < kept_counts[:, None]
    row_live = jnp.repeat(slot_live.reshape(SHARDS * MAXB), BLOCK)
    all_rows = jnp.concatenate([kept_rows, new_keyval], axis=0)
    all_live = jnp.concatenate([row_live, jnp.ones((TOKENS,), bool)])
    key_index = jnp.concatenate([jnp.full((SHARDS * MAXB * BLOCK,), -1, jnp.int32), jnp.arange(TOKENS).astype(jnp.int32)])
    head_group = QUERY_HEADS // KEYVALUE_HEADS

    def one_shard(shard):
        shard_queries = lax.dynamic_slice_in_dim(queries, (shard * TOK_DEV).astype(jnp.int32), TOK_DEV, 0)
        shard_queries = shard_queries.reshape(TOK_DEV, QUERY_HEADS, HEAD_WIDTH)
        query_index = shard * TOK_DEV + jnp.arange(TOK_DEV).astype(jnp.int32)
        visible = all_live[None, :] & (key_index[None, :] <= query_index[:, None])
        results = []
        for head_number in range(KEYVALUE_HEADS):
            head_queries = shard_queries[:, head_number * head_group:(head_number + 1) * head_group, :].astype(jnp.float32)
            keys_head = all_rows[:, head_number * 2 * HEAD_WIDTH:head_number * 2 * HEAD_WIDTH + HEAD_WIDTH].astype(jnp.float32)
            values_head = all_rows[:, head_number * 2 * HEAD_WIDTH + HEAD_WIDTH:(head_number + 1) * 2 * HEAD_WIDTH].astype(jnp.float32)
            scores = jnp.einsum('tgd,kd->tgk', head_queries, keys_head)
            masked = jnp.where(visible[:, None, :], scores, -1e+30)
            top = lax.optimization_barrier(jnp.max(masked, axis=-1, keepdims=True))
            weights = jnp.where(visible[:, None, :], jnp.exp(masked - top), 0.0)
            total = lax.optimization_barrier(jnp.sum(weights, axis=-1, keepdims=True))
            rounded = weights.astype(jnp.bfloat16).astype(jnp.float32)
            mixed = jnp.einsum('tgk,kd->tgd', rounded, values_head) / total
            results.append(mixed)
        return jnp.concatenate(results, axis=1).reshape(TOK_DEV, QUERY_HEADS * HEAD_WIDTH).astype(jnp.bfloat16)
    outputs = lax.map(one_shard, jnp.arange(SHARDS).astype(jnp.int32))
    return outputs.reshape(TOKENS, QUERY_HEADS * HEAD_WIDTH)
```

```python
import functools

import jax
import jax.numpy as jnp
from jax import lax
from jax.experimental import pallas as pl
from jax.experimental.pallas import tpu as pltpu
from jax.sharding import PartitionSpec as P

HEAD = 128
BLOCK = 128
MAXB = 3
GROUP = 8
TOK = 128
WIDTH = 8192
PEERS = 16
ROWS_SENT = MAXB * BLOCK + 16
KC = 512
RC = 256
NEG = -1e30

NT = (((1,), (1,)), ((), ()))
NN = (((1,), (0,)), ((), ()))


def plane_groups():
    return [[z * 8 + y * 4 + x for z in range(4) for x in range(4)] for y in range(2)]


def gather_plane(rows):
    copies = jnp.broadcast_to(rows[None], (PEERS,) + rows.shape)
    return lax.all_to_all(
        copies, "ctx", split_axis=0, concat_axis=0, axis_index_groups=plane_groups()
    )


def project_kernel(me_ref, tok_ref, gain_ref, ss_ref, wq_ref, wkv_ref, send_ref, keep_ref, normed):
    i, j = pl.program_id(0), pl.program_id(1)

    @pl.when((i == 0) & (j == 0))
    def _():
        scale = lax.rsqrt(ss_ref[...] * (1.0 / WIDTH) + 1e-05)
        values = tok_ref[...].astype(jnp.float32) * scale
        normed[...] = (values * gain_ref[...].astype(jnp.float32)).astype(jnp.bfloat16)

    q_part = jnp.dot(normed[...], wq_ref[...], preferred_element_type=jnp.float32)
    kv_part = jnp.dot(normed[...], wkv_ref[...], preferred_element_type=jnp.float32)
    for jj in range(2):

        @pl.when((i < 2) & (j == jj))
        def _():
            send_ref[0, :, jj * 512 : (jj + 1) * 512] = q_part
            send_ref[0, :, 1024 + jj * 128 : 1024 + (jj + 1) * 128] = kv_part

        @pl.when((i >= 2) & (j == jj))
        def _():
            keep_ref[0, :, jj * 512 : (jj + 1) * 512] = q_part
            keep_ref[0, :, 1024 + jj * 128 : 1024 + (jj + 1) * 128] = kv_part


def project(me, tokens, gain, sumsq, w_query, keyvalue_weight):
    def column(i, me_ref):
        rel = jnp.where(i == 0, 3, jnp.where(i == 1, 1, jnp.where(i == 2, 2, 0)))
        return me_ref[0] ^ rel

    shape = jax.ShapeDtypeStruct((2, TOK, 1280), jnp.float32)
    return pl.pallas_call(
        project_kernel,
        out_shape=(shape, shape),
        grid_spec=pltpu.PrefetchScalarGridSpec(
            num_scalar_prefetch=1,
            grid=(4, 2),
            in_specs=[
                pl.BlockSpec((TOK, 2048), lambda i, j, m: (0, 0)),
                pl.BlockSpec((1, 2048), lambda i, j, m: (0, 0)),
                pl.BlockSpec((TOK, 1), lambda i, j, m: (0, 0)),
                pl.BlockSpec((2048, 512), lambda i, j, m: (0, column(i, m) * 2 + j)),
                pl.BlockSpec((2048, 128), lambda i, j, m: (0, column(i, m) * 2 + j)),
            ],
            out_specs=[
                pl.BlockSpec((1, TOK, 1280), lambda i, j, m: (jnp.minimum(i, 1), 0, 0)),
                pl.BlockSpec((1, TOK, 1280), lambda i, j, m: (jnp.maximum(i - 2, 0), 0, 0)),
            ],
            scratch_shapes=[pltpu.VMEM((TOK, 2048), jnp.bfloat16)],
        ),
        compiler_params=pltpu.CompilerParams(vmem_limit_bytes=24 * 2**20),
        cost_estimate=pl.CostEstimate(
            flops=2 * TOK * 2048 * 5120, transcendentals=0, bytes_accessed=24 * 2**20
        ),
    )(me, tokens, gain.reshape(1, 2048), sumsq, w_query, keyvalue_weight)


def fold(q_ref, rows, first, kv, offset, top_ref, acc_ref, visible=None):
    keys = kv[pl.ds(offset, KC), 0:HEAD]
    values = kv[pl.ds(offset, KC), HEAD : 3 * HEAD]
    steps = rows // RC

    def score(r):
        s = lax.dot_general(
            q_ref[first + r * RC : first + (r + 1) * RC, :],
            keys,
            NT,
            preferred_element_type=jnp.float32,
        )
        return s if visible is None else jnp.where(visible, s, NEG)

    following = score(0)
    for r in range(steps):
        s = following
        if r + 1 < steps:
            following = score(r + 1)
        where = slice(first + r * RC, first + (r + 1) * RC)
        before = top_ref[where, :]
        top = jnp.maximum(before, jnp.max(s, axis=1, keepdims=True))
        weights = jnp.exp(s - top[:, 0:1])
        factor = jnp.exp(before - top)
        mixed = lax.dot_general(
            weights.astype(jnp.bfloat16), values, NN, preferred_element_type=jnp.float32
        )
        top_ref[where, :] = top
        acc_ref[where, 0:HEAD] = acc_ref[where, 0:HEAD] * factor + mixed[:, 0:HEAD]
        acc_ref[where, HEAD:] = acc_ref[where, HEAD:] * factor + mixed[:, HEAD:]


def stack_heads(q_ref, dst, first):
    for g in range(GROUP):
        dst[first + g * TOK : first + (g + 1) * TOK, :] = q_ref[:, g * HEAD : (g + 1) * HEAD]


def cached_kernel(counts_ref, qo_ref, qp_ref, kv_ref, acc_ref, top_ref, q_all, kv, sems):
    def copies(act):
        position = jnp.int32(0)
        for shard in range(PEERS):
            count = counts_ref[shard]
            for slot in range(MAXB):

                @pl.when(slot < count)
                def _():
                    act(
                        pltpu.make_async_copy(
                            kv_ref.at[shard, pl.ds(slot * BLOCK, BLOCK), :],
                            kv.at[pl.ds(pl.multiple_of((position + slot) * BLOCK, BLOCK), BLOCK), 0 : 2 * HEAD],
                            sems.at[shard * MAXB + slot],
                        )
                    )

            position = position + count
        return position

    live = copies(lambda c: c.start())
    for b in range(KC // BLOCK - 1):
        kv[pl.ds(pl.multiple_of((live + b) * BLOCK, BLOCK), BLOCK), 0 : 2 * HEAD] = jnp.zeros(
            (BLOCK, 2 * HEAD), jnp.bfloat16
        )
    kv[:, 2 * HEAD :] = jnp.ones((kv.shape[0], HEAD), jnp.bfloat16)
    stack_heads(qo_ref, q_all, 0)
    stack_heads(qp_ref, q_all, GROUP * TOK)
    top_ref[...] = jnp.full_like(top_ref, NEG)
    acc_ref[...] = jnp.zeros_like(acc_ref)
    copies(lambda c: c.wait())

    rows = 2 * GROUP * TOK
    chunks = (live * BLOCK + KC - 1) // KC

    def step(c, _):
        fold(q_all, rows, 0, kv, pl.multiple_of(c * KC, KC), top_ref, acc_ref)
        return 0

    lax.fori_loop(0, chunks - 1, step, 0)
    last = (chunks - 1) * KC
    column = lax.broadcasted_iota(jnp.int32, (RC, KC), 1)
    fold(q_all, rows, 0, kv, pl.multiple_of(last, KC), top_ref, acc_ref, column < live * BLOCK - last)


def attend_cached(counts, q_own, q_other, kv):
    rows = 2 * GROUP * TOK
    vmem = pl.BlockSpec(memory_space=pltpu.VMEM)
    return pl.pallas_call(
        cached_kernel,
        out_shape=(
            jax.ShapeDtypeStruct((rows, 2 * HEAD), jnp.float32),
            jax.ShapeDtypeStruct((rows, HEAD), jnp.float32),
        ),
        in_specs=[pl.BlockSpec(memory_space=pltpu.SMEM), vmem, vmem, pl.BlockSpec(memory_space=pl.ANY)],
        out_specs=(vmem, vmem),
        scratch_shapes=[
            pltpu.VMEM((rows, HEAD), jnp.bfloat16),
            pltpu.VMEM((PEERS * MAXB * BLOCK + KC, 3 * HEAD), jnp.bfloat16),
            pltpu.SemaphoreType.DMA((PEERS * MAXB,)),
        ],
        compiler_params=pltpu.CompilerParams(vmem_limit_bytes=40 * 2**20),
        cost_estimate=pl.CostEstimate(
            flops=4 * rows * 4096 * 256, transcendentals=rows * 4096, bytes_accessed=8 * 2**20
        ),
    )(counts, q_own, q_other, kv)


def span_kernel(own, info_ref, q_ref, kv_ref, acc_in, top_in, out_ref, log_ref, q_all, kv, acc, top, sems):
    chunks = info_ref[0]

    def copy(c):
        return pltpu.make_async_copy(
            kv_ref.at[pl.ds(c * KC, KC), :], kv.at[pl.ds(c * KC, KC), 0 : 2 * HEAD], sems.at[c]
        )

    last = chunks if own else chunks - 1
    for c in range(4):

        @pl.when(c <= last)
        def _():
            copy(c).start()

    kv[:, 2 * HEAD :] = jnp.ones((kv.shape[0], HEAD), jnp.bfloat16)
    stack_heads(q_ref, q_all, 0)
    acc[...] = acc_in[...]
    top[...] = top_in[...]
    for c in range(4):

        @pl.when(c <= last)
        def _():
            copy(c).wait()

    rows = GROUP * TOK

    def step(c, _):
        fold(q_all, rows, 0, kv, pl.multiple_of(c * KC, KC), top, acc)
        return 0

    lax.fori_loop(0, chunks, step, 0)
    if own:
        column = lax.broadcasted_iota(jnp.int32, (RC, KC), 1)
        token = lax.broadcasted_iota(jnp.int32, (RC, KC), 0) % TOK
        visible = column <= token + info_ref[1] * TOK
        fold(q_all, rows, 0, kv, pl.multiple_of(chunks * KC, KC), top, acc, visible)

    lane = lax.broadcasted_iota(jnp.int32, (TOK, HEAD), 1)
    logs = jnp.zeros((TOK, HEAD), jnp.float32)
    for g in range(GROUP):
        where = slice(g * TOK, (g + 1) * TOK)
        total = acc[where, HEAD:]
        out = acc[where, 0:HEAD] / total
        out_ref[:, g * HEAD : (g + 1) * HEAD] = out.astype(out_ref.dtype)
        log = top[where, :] + jnp.log(total)
        if own:
            logs = jnp.where(lane == g, log, logs)
        else:
            high = log.astype(jnp.bfloat16).astype(jnp.float32)
            middle = (log - high).astype(jnp.bfloat16).astype(jnp.float32)
            low = log - high - middle
            logs = jnp.where(lane == g, high, logs)
            logs = jnp.where(lane == GROUP + g, middle, logs)
            logs = jnp.where(lane == 2 * GROUP + g, low, logs)
    if own:
        log_ref[...] = logs
    else:
        out_ref[:, GROUP * HEAD :] = logs.astype(jnp.bfloat16)


def attend_span(own, info, q, kv, acc, top):
    rows = GROUP * TOK
    half = 0 if own else 1
    vmem = pl.BlockSpec(memory_space=pltpu.VMEM)
    if own:
        outs = (
            jax.ShapeDtypeStruct((TOK, GROUP * HEAD), jnp.float32),
            jax.ShapeDtypeStruct((TOK, HEAD), jnp.float32),
        )
        kernel = functools.partial(span_kernel, True)
    else:
        outs = (jax.ShapeDtypeStruct((TOK, (GROUP + 1) * HEAD), jnp.bfloat16),)

        def kernel(info_ref, q_ref, kv_ref, acc_in, top_in, out_ref, *scratch):
            span_kernel(False, info_ref, q_ref, kv_ref, acc_in, top_in, out_ref, None, *scratch)

    return pl.pallas_call(
        kernel,
        out_shape=outs,
        grid=(1,),
        in_specs=[
            pl.BlockSpec(memory_space=pltpu.SMEM),
            pl.BlockSpec((TOK, GROUP * HEAD), lambda i: (0, 0)),
            pl.BlockSpec(memory_space=pl.ANY),
            pl.BlockSpec((rows, 2 * HEAD), lambda i: (half, 0)),
            pl.BlockSpec((rows, HEAD), lambda i: (half, 0)),
        ],
        out_specs=tuple(pl.BlockSpec(o.shape, lambda i: (0, 0)) for o in outs),
        scratch_shapes=[
            pltpu.VMEM((rows, HEAD), jnp.bfloat16),
            pltpu.VMEM((4 * KC, 3 * HEAD), jnp.bfloat16),
            pltpu.VMEM((rows, 2 * HEAD), jnp.float32),
            pltpu.VMEM((rows, HEAD), jnp.float32),
            pltpu.SemaphoreType.DMA((4,)),
        ],
        compiler_params=pltpu.CompilerParams(vmem_limit_bytes=32 * 2**20),
        cost_estimate=pl.CostEstimate(
            flops=4 * rows * 2048 * 256, transcendentals=rows * 2048, bytes_accessed=4 * 2**20
        ),
    )(info, q, kv, acc, top)


def join_kernel(own_ref, log_ref, other_ref, out_ref):
    for g in range(GROUP):
        where = slice(g * HEAD, (g + 1) * HEAD)
        mine = log_ref[:, g : g + 1]
        base = GROUP * HEAD
        theirs = other_ref[:, base + g : base + g + 1].astype(jnp.float32)
        for part in (1, 2):
            at = base + part * GROUP + g
            theirs = theirs + other_ref[:, at : at + 1].astype(jnp.float32)
        share = 1.0 / (1.0 + jnp.exp(theirs - mine))
        rest = 1.0 / (1.0 + jnp.exp(mine - theirs))
        out = own_ref[:, where] * share + other_ref[:, where].astype(jnp.float32) * rest
        out_ref[:, where] = out.astype(jnp.bfloat16)


def join(own, logs, other):
    vmem = pl.BlockSpec(memory_space=pltpu.VMEM)
    return pl.pallas_call(
        join_kernel,
        out_shape=jax.ShapeDtypeStruct((TOK, GROUP * HEAD), jnp.bfloat16),
        in_specs=[vmem] * 3,
        out_specs=vmem,
    )(own, logs, other)


def on_device(tokens, norm_gain, w_query, keyvalue_weight, cache_keyval, kept_blocks, kept_counts):
    me = lax.axis_index("wa").astype(jnp.int32)
    shard = lax.axis_index("ctx").astype(jnp.int32)
    z, y_hi, x = shard // 8, (shard // 4) % 2, shard % 4

    kept = [
        lax.dynamic_slice_in_dim(cache_keyval, kept_blocks[0, s] * BLOCK, BLOCK, 0) for s in range(MAXB)
    ]
    count_rows = jnp.broadcast_to(kept_counts[0].astype(jnp.bfloat16), (16, 2 * HEAD))
    kept_all = gather_plane(jnp.concatenate([*kept, count_rows], axis=0))
    counts = kept_all[:, MAXB * BLOCK, 0].astype(jnp.int32)

    values = tokens.astype(jnp.float32)
    sumsq = lax.psum(jnp.sum(values * values, axis=1, keepdims=True), "wa")
    send, keep = project(me.reshape(1), tokens, norm_gain, sumsq, w_query, keyvalue_weight)
    got = lax.ppermute(send, "wa", [(i, i ^ 1) for i in range(4)])
    chip = keep + got
    far = lax.ppermute(chip[0], "wa", [(i, i ^ 2) for i in range(4)])
    whole = chip[1] + far
    queries = (whole[:, : GROUP * HEAD] * HEAD ** (-0.5)).astype(jnp.bfloat16)
    new_keyval = whole[:, GROUP * HEAD :].astype(jnp.bfloat16)

    across = [(i, i ^ 4) for i in range(32)]
    other_queries = lax.ppermute(queries, "ctx", across)
    new_all = gather_plane(new_keyval).reshape(PEERS * TOK, 2 * HEAD)

    acc, top = attend_cached(counts, queries, other_queries, kept_all)
    info_other = jnp.stack([z + 1 - y_hi, x])
    (sent,) = attend_span(False, info_other, other_queries, new_all, acc, top)
    theirs = lax.ppermute(sent, "ctx", across)
    info_own = jnp.stack([z, x])
    own, logs = attend_span(True, info_own, queries, new_all, acc, top)
    return join(own, logs, theirs)


def solution(mesh):
    return jax.shard_map(
        on_device,
        mesh=mesh,
        in_specs=(
            P("ctx", "wa"),
            P("wa"),
            P("wa", None),
            P("wa", None),
            P("ctx", "wa"),
            P("ctx", None),
            P("ctx"),
        ),
        out_specs=P("ctx", "wa"),
        check_vma=False,
    )
```
